512 devices in a mesh: grid: 64 (over x, z, core), mesh: 8 (over y).
Axes of the slice: x: 4, y: 8, z: 8, core: 2. Of those that a mesh axis runs over, the one named last changes fastest.
Arguments:
- grid_features: bfloat16 [474, 131072], P(None, ('grid', 'mesh')), may hold values from -6 to 6
- edge_feats: float32 [4, 262144], P(None, ('grid', 'mesh')), may hold values from -6 to 6
- edge_src: int32 [262144], P(('grid', 'mesh')), may hold values from 0 to 255, as said below
- edge_dst: int32 [262144], P(('grid', 'mesh')), may hold values from 0 to 65535, as said below
- edge_count: int32 [512], P(('grid', 'mesh')), may hold values from 16 to 512, as said below
- mesh_lat: bfloat16 [65536, 512], P(('grid', 'mesh')), may hold values from -6 to 6
- owner_map: int32 [65536], P(('grid', 'mesh')), may hold values from 0 to 65535, as said below
- w_grid: bfloat16 [474, 512], replicated, may hold values from -0.25 to 0.25
- w_edge: float32 [4, 512], replicated, may hold values from -3 to 3
- w_msg_in: bfloat16 [1024, 512], replicated, may hold values from -0.1875 to 0.1875
- w_msg_out: bfloat16 [512, 512], replicated, may hold values from -0.25 to 0.25
- gain_msg: float32 [512], replicated, may hold values from 0.5 to 1.5
- w_node_in: bfloat16 [1024, 512], replicated, may hold values from -0.1875 to 0.1875
- w_node_out: bfloat16 [512, 512], replicated, may hold values from -0.25 to 0.25
- gain_node: float32 [512], replicated, may hold values from 0.5 to 1.5
Outputs:
- mesh_out: bfloat16 [65536, 512], P(('grid', 'mesh'))
The draws below stay inside these ranges and needn't reach their ends.
Inputs may be any that keep to these rules, and one draw needn't show every extreme that they name: `edge_src`: index among the 256 grid nodes of the device that holds the edge; 0 on slots that are not live. `edge_dst`: live slots of a device come first and are sorted by destination, and every destination lies on an owner with the device's own mesh index; slots that are not live hold 0. From one device, at most 16 live edges go to one owner and they reach at most 4 distinct positions; for each mesh index one owner receives exactly 16 live edges over exactly 4 positions from every device of that mesh index. `edge_count`: number of live slots of each device; in every draw some device has all 512 slots live. `owner_map`: A permutation; the positions of an aligned block of 8 * 128 positions (one grid index) hold the nodes of the same block, and each owner holds exactly 128 / 8 nodes of each device of its grid index.
All inputs are finite; a program needn't handle non-finite values.
Results may differ from the reference program's by a relative error of at most 0.005.
Values may be sent and summed in bfloat16 or wider, within the bound.
A program may use at most 64 MiB of HBM per device.

```python
import jax
import jax.numpy as jnp
from jax import lax

LAT = 512
CH = 474
EF = 4
G_DEV = 256
MN_DEV = 128
E_DEV = 512
CAP_E = 16
CAP_N = 4
GRID_NODES = 131072
EDGES = 262144
MESH_NODES = 65536
N_GRID = 64
N_MESH = 8


def device_edges(key):
    devices = N_GRID * N_MESH
    key_list = jax.random.split(jax.random.fold_in(key, 11), 6)
    full_device = jax.random.randint(jax.random.fold_in(key, 23), (), 0, devices)
    hot_owner = jax.random.randint(key_list[0], (N_MESH,), 0, N_GRID)
    empty_shift = jax.random.randint(key_list[1], (devices,), 1, N_GRID)
    device_ids = jnp.arange(devices, dtype=jnp.int32)
    mesh_column = device_ids % N_MESH
    busiest = hot_owner[mesh_column]
    emptied = (busiest + empty_shift) % N_GRID
    owner_ids = jnp.arange(N_GRID, dtype=jnp.int32)
    block_counts = jax.random.randint(key_list[2], (devices, N_GRID), 0, CAP_E // 2 + 1)
    block_counts = jnp.where((device_ids == full_device)[:, None], CAP_E // 2, block_counts)
    block_counts = jnp.where(owner_ids[None, :] == busiest[:, None], CAP_E, block_counts)
    block_counts = jnp.where(owner_ids[None, :] == emptied[:, None], 0, block_counts)
    extra_picks = jax.random.randint(key_list[3], (devices, N_GRID, CAP_E - CAP_N), 0, CAP_N)
    forced_picks = jnp.broadcast_to(jnp.arange(CAP_N, dtype=jnp.int32), (devices, N_GRID, CAP_N))
    node_picks = jnp.sort(jnp.concatenate([forced_picks, extra_picks], axis=2), axis=2)
    scores = jax.random.randint(key_list[4], (devices, N_GRID, MN_DEV), 0, 1 << 20) * MN_DEV + jnp.arange(MN_DEV, dtype=jnp.int32)
    chosen = jnp.sort(jnp.argsort(scores, axis=2)[:, :, :CAP_N], axis=2).astype(jnp.int32)
    picked_nodes = jnp.take_along_axis(chosen, node_picks, axis=2)
    positions = (owner_ids[None, :, None] * N_MESH + mesh_column[:, None, None]) * MN_DEV + picked_nodes
    positions = positions.reshape(devices, N_GRID * CAP_E)
    block_ends = jnp.cumsum(block_counts, axis=1)
    block_starts = block_ends - block_counts
    slot_ids = jnp.arange(E_DEV, dtype=jnp.int32)

    def pack_device(operands):
        ends_row, starts_row, positions_row = operands
        owner_of = jnp.sum((ends_row[None, :] <= slot_ids[:, None]).astype(jnp.int32), axis=1)
        owner_of = jnp.minimum(owner_of, N_GRID - 1)
        block_offset = slot_ids - starts_row[owner_of]
        is_live = slot_ids < ends_row[N_GRID - 1]
        lookup = jnp.where(is_live, owner_of * CAP_E + block_offset, 0)
        return jnp.where(is_live, positions_row[lookup], 0)
    destinations = lax.map(pack_device, (block_ends, block_starts, positions))
    live_counts = block_ends[:, N_GRID - 1]
    sources = jax.random.randint(key_list[5], (devices, E_DEV), 0, G_DEV)
    sources = jnp.where(slot_ids[None, :] < live_counts[:, None], sources, 0)
    return (destinations.reshape(-1).astype(jnp.int32), sources.reshape(-1).astype(jnp.int32), live_counts.astype(jnp.int32))


def draw_edge_dst(key, part):
    shared = device_edges(key)
    return shared[0]


def draw_edge_src(key, part):
    shared = device_edges(key)
    return shared[1]


def draw_edge_count(key, part):
    shared = device_edges(key)
    return shared[2]


def draw_owner_map(key, part):
    key = jax.random.fold_in(key, 5)
    first_key, second_key = jax.random.split(key)
    share = MN_DEV // N_MESH
    node_ids = (jnp.arange(N_GRID, dtype=jnp.int32)[:, None, None] * N_MESH + jnp.arange(N_MESH, dtype=jnp.int32)[None, :, None]) * MN_DEV + jnp.arange(MN_DEV, dtype=jnp.int32)[None, None, :]
    node_ids = jax.random.permutation(first_key, node_ids, axis=2, independent=True)
    node_ids = node_ids.reshape(N_GRID, N_MESH, N_MESH, share)
    node_ids = jnp.transpose(node_ids, (0, 2, 1, 3)).reshape(N_GRID, N_MESH, MN_DEV)
    node_ids = jax.random.permutation(second_key, node_ids, axis=2, independent=True)
    return node_ids.reshape(-1).astype(jnp.int32)


def steps_of(rng, extent, cuts, least, top_value):
    def one(axis_at, blocks):
        steps = jax.random.uniform(jax.random.fold_in(jax.random.fold_in(rng, 6), axis_at), (blocks,), jnp.float32, least / len(cuts), top_value / len(cuts))
        return jnp.repeat(jnp.exp(steps), extent[axis_at] // blocks).reshape((-1,) + (1,) * (len(extent) - axis_at - 1))

    level = one(*cuts[0])
    for cut in cuts[1:]:
        level = level * one(*cut)
    return level


def gaussian(rng, extent, deviation, bound, cuts=(), held_as=jnp.bfloat16):
    level = steps_of(rng, extent, cuts, -0.22, 0.18) if cuts else 1.0
    values = jax.random.normal(rng, extent, jnp.float32) * deviation * level
    return jnp.minimum(jnp.maximum(values, -bound), bound).astype(held_as)


def setup_inputs(seed: int = 0) -> dict:
    splits = jax.random.split(jax.random.key(seed), 16)
    return {
        "grid_features": gaussian(splits[0], (CH, GRID_NODES), 1.0, 6.0, ((1, 512),)),
        "edge_feats": gaussian(splits[1], (EF, EDGES), 1.0, 6.0, ((1, 512),), jnp.float32),
        "edge_src": draw_edge_src(jax.random.fold_in(splits[15], 71), 0),
        "edge_dst": draw_edge_dst(jax.random.fold_in(splits[15], 71), 0),
        "edge_count": draw_edge_count(jax.random.fold_in(splits[15], 71), 0),
        "mesh_lat": gaussian(splits[5], (MESH_NODES, LAT), 1.0, 6.0, ((0, 512),)),
        "owner_map": draw_owner_map(jax.random.fold_in(splits[15], 71), 0),
        "w_grid": gaussian(splits[7], (CH, LAT), CH ** -0.5, 0.25),
        "w_edge": gaussian(splits[8], (EF, LAT), EF ** -0.5, 3.0, (), jnp.float32),
        "w_msg_in": gaussian(splits[9], (2 * LAT, LAT), (2 * LAT) ** -0.5, 0.1875),
        "w_msg_out": gaussian(splits[10], (LAT, LAT), LAT ** -0.5, 0.25),
        "gain_msg": jnp.clip(1.0 + 0.1 * jax.random.normal(splits[11], (LAT,), jnp.float32), 0.5, 1.5),
        "w_node_in": gaussian(splits[12], (2 * LAT, LAT), (2 * LAT) ** -0.5, 0.1875),
        "w_node_out": gaussian(splits[13], (LAT, LAT), LAT ** -0.5, 0.25),
        "gain_node": jnp.clip(1.0 + 0.1 * jax.random.normal(splits[14], (LAT,), jnp.float32), 0.5, 1.5),
    }


def layer_norm(values, scaling):
    row_mean = lax.optimization_barrier(jnp.mean(values, axis=-1, keepdims=True))
    centred = values - row_mean
    variance = lax.optimization_barrier(jnp.mean(centred * centred, axis=-1, keepdims=True))
    return centred * lax.rsqrt(variance + 1e-05) * scaling

def edge_messages(features, edge_part, sources, live_count, w_grid, w_edge, w_msg_in, w_msg_out, gain_msg):
    grid_latent = jax.nn.silu(lax.dot_general(features, w_grid, (((0,), (0,)), ((), ())), preferred_element_type=jnp.float32)).astype(jnp.bfloat16)
    edge_latent = jax.nn.silu(lax.dot_general(edge_part, w_edge, (((0,), (0,)), ((), ())), precision=lax.Precision.HIGHEST, preferred_element_type=jnp.float32)).astype(jnp.bfloat16)
    sender_latent = jnp.take(grid_latent, sources, axis=0)
    latent_width = w_msg_out.shape[0]
    preactivation = jnp.dot(edge_latent, w_msg_in[:latent_width], preferred_element_type=jnp.float32) + jnp.dot(sender_latent, w_msg_in[latent_width:], preferred_element_type=jnp.float32)
    hidden_edge = jax.nn.silu(preactivation).astype(jnp.bfloat16)
    mixed = jnp.dot(hidden_edge, w_msg_out, preferred_element_type=jnp.float32)
    is_live = jnp.arange(sources.shape[0], dtype=jnp.int32) < live_count
    renewed = edge_latent.astype(jnp.float32) + layer_norm(mixed, gain_msg)
    return jnp.where(is_live[:, None], renewed, jnp.zeros_like(renewed)).astype(jnp.bfloat16)

def reference(grid_features, edge_feats, edge_src, edge_dst, edge_count, mesh_lat, owner_map, w_grid, w_edge, w_msg_in, w_msg_out, gain_msg, w_node_in, w_node_out, gain_node):

    def accumulate(message_sum, device_index):
        grid_start = (device_index * G_DEV).astype(jnp.int32)
        edge_start = (device_index * E_DEV).astype(jnp.int32)
        features = lax.dynamic_slice_in_dim(grid_features, grid_start, G_DEV, 1)
        edge_part = lax.dynamic_slice_in_dim(edge_feats, edge_start, E_DEV, 1)
        sources = lax.dynamic_slice_in_dim(edge_src, edge_start, E_DEV, 0)
        targets = lax.dynamic_slice_in_dim(edge_dst, edge_start, E_DEV, 0)
        live_count = lax.dynamic_index_in_dim(edge_count, device_index, 0, keepdims=False)
        message = edge_messages(features, edge_part, sources, live_count, w_grid, w_edge, w_msg_in, w_msg_out, gain_msg)
        return (message_sum.at[targets].add(message.astype(jnp.float32)), None)
    message_sum, unused = lax.scan(accumulate, jnp.zeros((MESH_NODES, LAT), jnp.float32), jnp.arange(N_GRID * N_MESH, dtype=jnp.int32))
    summed_low = message_sum.astype(jnp.bfloat16)
    preactivation = jnp.dot(mesh_lat, w_node_in[:LAT], preferred_element_type=jnp.float32) + jnp.dot(summed_low, w_node_in[LAT:], preferred_element_type=jnp.float32)
    hidden_node = jax.nn.silu(preactivation).astype(jnp.bfloat16)
    mixed = jnp.dot(hidden_node, w_node_out, preferred_element_type=jnp.float32)
    renewed = (mesh_lat.astype(jnp.float32) + layer_norm(mixed, gain_node)).astype(jnp.bfloat16)
    return jnp.zeros_like(renewed).at[owner_map].set(renewed)
```

```python
import functools

import jax
import jax.numpy as jnp
from jax import lax
from jax.experimental import pallas as pl
from jax.experimental.pallas import tpu as pltpu
from jax.sharding import PartitionSpec as P

F32 = jnp.float32
BF16 = jnp.bfloat16
MESH = pl.DeviceIdType.MESH
CAP = 4
TILE = 16
LOG_CORES = 1
LOG_RING = 3
CORES = 1 << LOG_CORES
RING = 1 << LOG_RING


def far_first(size):
    return sorted(range(1, size), key=lambda step: -min(step, size - step))


def silu(v):
    half = 0.5 * v
    return half + half * jnp.tanh(half)


def normed(v):
    mean = jnp.mean(v, axis=-1, keepdims=True)
    centred = v - mean
    variance = jnp.mean(centred * centred, axis=-1, keepdims=True)
    return centred * lax.rsqrt(variance + 1e-05)


def dot(a, b):
    return lax.dot_general(a, b, (((1,), (0,)), ((), ())), preferred_element_type=F32)


def dot_tn(a, b):
    return lax.dot_general(a, b, (((0,), (0,)), ((), ())), preferred_element_type=F32)


def dot_nt(a, b):
    return lax.dot_general(a, b, (((1,), (1,)), ((), ())), preferred_element_type=F32)


def iota(shape, dim):
    return lax.broadcasted_iota(jnp.int32, shape, dim)


def hot(mask):
    return jnp.where(mask, 1.0, 0.0).astype(BF16)


def parts(v):
    a = v.astype(BF16).astype(F32)
    rest = v - a
    b = rest.astype(BF16).astype(F32)
    return a, b, rest - b


def kernel(
    groups,
    columns,
    feat_h,
    ef_h,
    src_h,
    dst_h,
    lat_h,
    map_h,
    w_grid_h,
    w_edge_h,
    w_mi_h,
    w_mo_h,
    gain_m_h,
    w_ni_h,
    w_no_h,
    gain_n_h,
    out_ref,
    feat,
    ef,
    src,
    dst,
    lat,
    omap,
    w_grid,
    w_edge,
    w_mi,
    w_mo,
    gain_m,
    w_ni,
    w_no,
    gain_n,
    message,
    wide,
    send,
    recv,
    id_send,
    id_passed,
    id_recv,
    adding,
    place_send,
    place_recv,
    row_send,
    row_recv,
    load_sem,
    id_sems,
    id_sems_2,
    place_sems,
    pay_sems,
    row_sems,
):
    width = w_mo.shape[0]
    slots = dst.shape[1]
    nodes = omap.shape[1]
    g_nodes = feat.shape[1]
    me = lax.axis_index("grid")
    my = lax.axis_index("mesh")

    loads = {}
    pairs = (
        (dst_h, dst),
        (src_h, src),
        (ef_h, ef),
        (w_edge_h, w_edge),
        (feat_h, feat),
        (w_grid_h, w_grid),
        (w_mi_h, w_mi),
        (w_mo_h, w_mo),
        (gain_m_h, gain_m),
        (map_h, omap),
        (lat_h, lat),
        (w_ni_h, w_ni),
        (w_no_h, w_no),
        (gain_n_h, gain_n),
    )
    for at, (here, there) in enumerate(pairs):
        loads[id(there)] = pltpu.make_async_copy(here, there, load_sem.at[at])
    for there in (dst, omap, src, ef, w_edge, feat, w_grid, w_mi, w_mo, gain_m):
        loads[id(there)].start()

    def ready(*refs):
        for ref in refs:
            loads[id(ref)].wait()

    depth = groups // CORES // RING
    spokes = depth * CORES
    core = lax.rem(me, CORES)
    ring_at = lax.rem(lax.div(me, CORES), RING)
    spoke_at = lax.div(me, CORES * RING) * CORES + core

    def ring_peer(step):
        at = lax.rem(ring_at + step, RING)
        return at, me + (at - ring_at) * CORES

    def spoke_peer(step):
        at = lax.rem(spoke_at + step, spokes)
        return at, (lax.div(at, CORES) * RING + ring_at) * CORES + lax.rem(at, CORES)

    ring_steps = far_first(RING)
    spoke_steps = far_first(spokes)
    mesh_steps = far_first(columns)
    barrier = pltpu.get_barrier_semaphore()

    def ring_turn(turn):
        step = lax.div(RING - turn, 2) * (1 - 2 * lax.rem(turn, 2))
        return lax.rem(ring_at + step + RING, RING)

    def greet(peer):
        pl.semaphore_signal(barrier, inc=1, device_id={"grid": peer}, device_id_type=MESH)

    def greet_ring(turn, carry):
        at = ring_turn(turn)
        for spoke in range(spokes):
            greet((spoke // CORES * RING + at) * CORES + spoke % CORES)
        return carry

    lax.fori_loop(0, RING - 1, greet_ring, 0)
    for step in spoke_steps:
        greet(spoke_peer(step)[1])
    for step in mesh_steps:
        to = {"mesh": lax.rem(my + step, columns)}
        pl.semaphore_signal(barrier, inc=1, device_id=to, device_id_type=MESH)

    shift = (nodes * columns).bit_length() - 1
    upto = hot(iota((slots, slots), 0) <= iota((slots, slots), 1))
    ready(dst, omap, src, ef, w_edge)
    target = jnp.broadcast_to(dst[...], (8, slots))
    edge_at = iota((8, slots), 1)
    last = jnp.max(jnp.where(target > 0, edge_at, -1), axis=1, keepdims=True)
    live = edge_at <= last
    fresh = live & ((edge_at == 0) | (target != pltpu.roll(target, 1, 1)))
    fresh_f = jnp.where(fresh, 1.0, 0.0)
    band = lax.shift_right_logical(target, shift)
    low = band & (CORES - 1)
    along = lax.shift_right_logical(band, LOG_CORES) & (RING - 1)
    across = lax.shift_right_logical(band, LOG_CORES + LOG_RING)
    owner = jnp.where(live, along * spokes + across * CORES + low, -1)
    of_owner = owner[0:1] == iota((groups, slots), 0)
    counted = dot(jnp.where(of_owner, fresh_f[0:1], 0.0).astype(BF16), upto)
    rank = jnp.sum(jnp.where(of_owner, counted, 0.0), axis=0, keepdims=True)
    row_of_edge = jnp.where(
        live[0:1], (rank.astype(jnp.int32) - 1) * groups + owner[0:1], -1
    )
    picking = hot(row_of_edge == iota((CAP * groups, slots), 0))
    local_f = jnp.where(fresh, (target & (nodes - 1)).astype(F32), 0.0)
    ids = dot_nt(picking, jnp.broadcast_to(local_f[0:1], (128, slots)).astype(BF16))
    lane = iota((groups, 128), 1)
    keys = ids[0:groups]
    for j in range(1, CAP):
        keys = jnp.where(lane & (CAP - 1) == j, ids[j * groups : (j + 1) * groups], keys)
    id_send[...] = keys.reshape(RING, spokes, 1, 128)

    share = nodes // columns
    node_shift = nodes.bit_length() - 1
    held = omap[...]
    home = lax.shift_right_logical(held, node_shift) & (columns - 1)
    at_home = home == iota((columns, nodes), 0)
    before = hot(iota((nodes, nodes), 0) <= iota((nodes, nodes), 1))
    nth = dot(hot(at_home), before)
    leave = jnp.sum(
        jnp.where(at_home, nth + (iota((columns, nodes), 0) * share - 1).astype(F32), 0.0),
        axis=0,
        keepdims=True,
    )
    leaving = hot(leave.astype(jnp.int32) == iota((nodes, nodes), 0))
    node_hot_t = hot((held & (nodes - 1)) == iota((nodes, nodes), 0))
    place_send[...] = dot_nt(leaving, node_hot_t).astype(BF16)
    position = dot_nt(
        leaving, jnp.broadcast_to(iota((1, nodes), 1).astype(F32), (128, nodes)).astype(BF16)
    )

    ready(feat, w_grid)
    e1, e2, e3 = parts(ef[...])
    w1, w2, w3 = parts(w_edge[...])
    e_all = jnp.concatenate([e1, e1, e2, e1, e2, e3], axis=0).astype(BF16)
    w_all = jnp.concatenate([w1, w2, w1, w3, w2, w1], axis=0).astype(BF16)
    edge_latent = silu(dot_tn(e_all, w_all)).astype(BF16)
    grid_latent = silu(dot_tn(feat[...], w_grid[...])).astype(BF16)
    from_node = jnp.transpose(jnp.broadcast_to(src[...], (128, slots)))
    gathering = [hot(from_node == iota((slots, 128), 1) + at) for at in range(0, g_nodes, 128)]
    ready(w_mi)
    w_mi[width : width + g_nodes] = dot(grid_latent, w_mi[width:]).astype(BF16)
    both = jnp.concatenate([edge_latent] + gathering, axis=1)
    hidden = silu(dot(both, w_mi[0 : width + g_nodes])).astype(BF16)
    ready(w_mo, gain_m)
    for there in (lat, w_ni, w_no, gain_n):
        loads[id(there)].start()
    mixed = dot(hidden, w_mo[...])
    message[...] = (edge_latent.astype(F32) + normed(mixed) * gain_m[...]).astype(BF16)
    summed = dot(picking, message[...])
    quarters = width // 128
    for j in range(CAP):
        for c in range(quarters):
            wide[pl.ds(j * quarters + c, groups, stride=TILE), :] = summed[
                j * groups : (j + 1) * groups, c * 128 : (c + 1) * 128
            ]
    send[...] = wide[...].astype(BF16).reshape(groups, TILE, 128)
    pl.semaphore_wait(barrier, groups + columns - 2)

    def remote(outgoing, incoming, sems, to):
        return pltpu.make_async_remote_copy(
            src_ref=outgoing,
            dst_ref=incoming,
            send_sem=sems.at[0],
            recv_sem=sems.at[1],
            device_id=to,
            device_id_type=MESH,
        )

    def along_ring(outgoing, incoming, sems):
        for step in ring_steps:
            at, peer = ring_peer(step)
            remote(outgoing.at[at], incoming.at[ring_at], sems, {"grid": peer}).start()
        incoming[pl.ds(ring_at, 1)] = outgoing[pl.ds(ring_at, 1)]

    def along_spokes(outgoing, incoming, sems):
        for step in spoke_steps:
            at, peer = spoke_peer(step)
            remote(outgoing.at[:, at], incoming.at[spoke_at], sems, {"grid": peer}).start()
        kept = outgoing[:, pl.ds(spoke_at, 1)]
        incoming[pl.ds(spoke_at, 1)] = kept.reshape((1, RING) + kept.shape[2:])

    def along_mesh(outgoing, incoming, sems):
        def rows(at):
            return pl.ds(pl.multiple_of(at * share, share), share)

        for step in mesh_steps:
            peer = lax.rem(my + step, columns)
            remote(outgoing.at[rows(peer)], incoming.at[rows(my)], sems, {"mesh": peer}).start()
        incoming[rows(my), :] = outgoing[rows(my), :]

    def drain(sem, ref):
        pltpu.make_async_copy(ref, ref, sem).wait()

    slot = spoke_at * RING + ring_at

    along_ring(id_send, id_passed, id_sems)

    def pay_ring(turn, carry):
        at = ring_turn(turn)
        for spoke_step in range(spokes):
            spoke = lax.rem(spoke_at + spoke_step, spokes)
            peer = (lax.div(spoke, CORES) * RING + at) * CORES + lax.rem(spoke, CORES)
            block = send.at[at * spokes + spoke]
            remote(block, recv.at[slot], pay_sems, {"grid": peer}).start()
        return carry

    lax.fori_loop(0, RING - 1, pay_ring, 0)
    for step in spoke_steps:
        at, peer = spoke_peer(step)
        block = send.at[ring_at * spokes + at]
        remote(block, recv.at[slot], pay_sems, {"grid": peer}).start()
    recv[pl.ds(slot, 1)] = send[pl.ds(ring_at * spokes + spoke_at, 1)]
    drain(id_sems.at[1], id_passed.at[pl.ds(0, RING - 1)])
    along_spokes(id_passed, id_recv, id_sems_2)

    along_mesh(place_send, place_recv, place_sems)

    ready(lat, w_ni)
    lat_rows = dot(leaving, lat[...])
    pre = dot(lat_rows.astype(BF16), w_ni[0:width])
    drain(id_sems_2.at[1], id_recv.at[pl.ds(0, spokes - 1)])
    lines = id_recv[...].reshape(groups, 128)
    senders = 128 // CAP
    mine = lax.shift_right_logical(iota((senders, 128), 1), CAP.bit_length() - 1) == iota(
        (senders, 128), 0
    )
    for b in range(groups // senders):
        key = jnp.sum(
            jnp.where(mine, lines[b * senders : (b + 1) * senders], 0.0), axis=0, keepdims=True
        )
        adding[:, b * 128 : (b + 1) * 128] = hot(key == position)
    drain(place_sems.at[1], place_recv.at[pl.ds(0, nodes - share)])
    placing = jnp.transpose(place_recv[...].astype(F32)).astype(BF16)
    ready(w_no, gain_n)

    drain(pay_sems.at[1], recv.at[pl.ds(0, groups - 1)])
    wide[...] = recv[...].reshape(groups * TILE, 128).astype(F32)
    rows = jnp.concatenate(
        [wide[pl.ds(c, CAP * groups, stride=quarters), :].astype(BF16) for c in range(quarters)],
        axis=1,
    )
    summed_low = dot(adding[...], rows).astype(BF16)
    hidden_node = silu(pre + dot(summed_low, w_ni[width:])).astype(BF16)
    mixed_node = dot(hidden_node, w_no[...])
    row_send[...] = (lat_rows + normed(mixed_node) * gain_n[...]).astype(BF16)

    along_mesh(row_send, row_recv, row_sems)
    drain(id_sems.at[0], id_send.at[pl.ds(0, RING - 1)])
    drain(id_sems_2.at[0], id_recv.at[pl.ds(0, spokes - 1)])
    drain(place_sems.at[0], place_send.at[pl.ds(0, nodes - share)])
    drain(pay_sems.at[0], send.at[pl.ds(0, groups - 1)])
    drain(row_sems.at[1], row_recv.at[pl.ds(0, nodes - share)])
    out_ref[...] = dot(placing, row_recv[...]).astype(BF16)
    drain(row_sems.at[0], row_send.at[pl.ds(0, nodes - share)])


def shards(
    grid_features,
    edge_feats,
    edge_src,
    edge_dst,
    edge_count,
    mesh_lat,
    owner_map,
    w_grid,
    w_edge,
    w_msg_in,
    w_msg_out,
    gain_msg,
    w_node_in,
    w_node_out,
    gain_node,
):
    groups, columns = lax.axis_size("grid"), lax.axis_size("mesh")
    nodes, width = mesh_lat.shape
    operands = (
        grid_features,
        edge_feats,
        edge_src.reshape(1, -1),
        edge_dst.reshape(1, -1),
        mesh_lat,
        owner_map.reshape(1, -1),
        w_grid,
        w_edge,
        w_msg_in,
        w_msg_out,
        gain_msg.reshape(1, -1),
        w_node_in,
        w_node_out,
        gain_node.reshape(1, -1),
    )
    copies = [pltpu.VMEM(v.shape, v.dtype) for v in operands]
    rows = groups * TILE
    spokes = groups // RING
    return pl.pallas_call(
        functools.partial(kernel, groups, columns),
        out_shape=pltpu.VMEM((nodes, width), BF16),
        in_specs=[pl.BlockSpec(memory_space=pl.ANY)] * len(operands),
        out_specs=pl.BlockSpec(memory_space=pltpu.VMEM),
        scratch_shapes=copies
        + [
            pltpu.VMEM((edge_dst.shape[0], width), BF16),
            pltpu.VMEM((rows, 128), F32),
            pltpu.VMEM((groups, TILE, 128), BF16),
            pltpu.VMEM((groups, TILE, 128), BF16),
            pltpu.VMEM((RING, spokes, 1, 128), F32),
            pltpu.VMEM((RING, spokes, 1, 128), F32),
            pltpu.VMEM((spokes, RING, 1, 128), F32),
            pltpu.VMEM((nodes, CAP * groups), BF16),
            pltpu.VMEM((nodes, nodes), BF16),
            pltpu.VMEM((nodes, nodes), BF16),
            pltpu.VMEM((nodes, width), BF16),
            pltpu.VMEM((nodes, width), BF16),
            pltpu.SemaphoreType.DMA((len(operands),)),
        ]
        + [pltpu.SemaphoreType.DMA((2,))] * 5,
        compiler_params=pltpu.CompilerParams(
            collective_id=0, has_side_effects=True, vmem_limit_bytes=56 * 1024 * 1024
        ),
        cost_estimate=pl.CostEstimate(
            flops=2_000_000_000, bytes_accessed=5_000_000, transcendentals=800_000
        ),
        name="encode",
    )(*operands)


def solution(mesh):
    placed = (
        P(None, ("grid", "mesh")),
        P(None, ("grid", "mesh")),
        P(("grid", "mesh")),
        P(("grid", "mesh")),
        P(("grid", "mesh")),
        P(("grid", "mesh"), None),
        P(("grid", "mesh")),
        P(),
        P(),
        P(),
        P(),
        P(),
        P(),
        P(),
        P(),
    )
    return jax.shard_map(
        shards, mesh=mesh, in_specs=placed, out_specs=P(("grid", "mesh"), None), check_vma=False
    )
```

```python
import functools

import jax
import jax.numpy as jnp
from jax import lax
from jax.experimental import pallas as pl
from jax.experimental.pallas import tpu as pltpu
from jax.sharding import PartitionSpec as P

F32 = jnp.float32
BF16 = jnp.bfloat16
MESH = pl.DeviceIdType.MESH
CAP = 4
TILE = 16
LOG_CORES = 1
LOG_RING = 3
CORES = 1 << LOG_CORES
RING = 1 << LOG_RING


def far_first(size):
    return sorted(range(1, size), key=lambda step: -min(step, size - step))


def silu(v):
    half = 0.5 * v
    return half + half * jnp.tanh(half)


def normed(v):
    mean = jnp.mean(v, axis=-1, keepdims=True)
    centred = v - mean
    variance = jnp.mean(centred * centred, axis=-1, keepdims=True)
    return centred * lax.rsqrt(variance + 1e-05)


def dot(a, b):
    return lax.dot_general(a, b, (((1,), (0,)), ((), ())), preferred_element_type=F32)


def dot_tn(a, b):
    return lax.dot_general(a, b, (((0,), (0,)), ((), ())), preferred_element_type=F32)


def dot_nt(a, b):
    return lax.dot_general(a, b, (((1,), (1,)), ((), ())), preferred_element_type=F32)


def iota(shape, dim):
    return lax.broadcasted_iota(jnp.int32, shape, dim)


def hot(mask):
    return jnp.where(mask, 1.0, 0.0).astype(BF16)


def hot_rows(row, count):
    at = iota((count, row.shape[1]), 0).astype(F32).astype(BF16)
    there = jnp.broadcast_to(row.astype(BF16), at.shape)
    return jnp.where(there == at, jnp.ones_like(at), jnp.zeros_like(at))


def parts(v):
    a = v.astype(BF16).astype(F32)
    rest = v - a
    b = rest.astype(BF16).astype(F32)
    return a, b, rest - b


def kernel(
    groups,
    columns,
    feat_h,
    ef_h,
    src_h,
    dst_h,
    lat_h,
    map_h,
    w_grid_h,
    w_edge_h,
    w_mi_h,
    w_mo_h,
    gain_m_h,
    w_ni_h,
    w_no_h,
    gain_n_h,
    out_ref,
    feat,
    ef,
    src,
    dst,
    lat,
    omap,
    w_grid,
    w_edge,
    w_mi,
    w_mo,
    gain_m,
    w_ni,
    w_no,
    gain_n,
    message,
    wide,
    send,
    recv,
    id_send,
    id_passed,
    id_recv,
    adding,
    place_send,
    place_recv,
    row_send,
    row_recv,
    load_sem,
    id_sems,
    id_sems_2,
    place_sems,
    pay_sems,
    row_sems,
):
    width = w_mo.shape[0]
    slots = dst.shape[1]
    nodes = omap.shape[1]
    g_nodes = feat.shape[1]
    me = lax.axis_index("grid")
    my = lax.axis_index("mesh")

    loads = {}
    pairs = (
        (dst_h, dst),
        (src_h, src),
        (ef_h, ef),
        (w_edge_h, w_edge),
        (feat_h, feat),
        (w_grid_h, w_grid),
        (w_mi_h, w_mi),
        (w_mo_h, w_mo),
        (gain_m_h, gain_m),
        (map_h, omap),
        (lat_h, lat),
        (w_ni_h, w_ni),
        (w_no_h, w_no),
        (gain_n_h, gain_n),
    )
    for at, (here, there) in enumerate(pairs):
        loads[id(there)] = pltpu.make_async_copy(here, there, load_sem.at[at])
    for there in (dst, src, ef, w_edge, feat, w_grid, w_mi, w_mo, gain_m):
        loads[id(there)].start()

    def ready(*refs):
        for ref in refs:
            loads[id(ref)].wait()

    depth = groups // CORES // RING
    spokes = depth * CORES
    core = lax.rem(me, CORES)
    ring_at = lax.rem(lax.div(me, CORES), RING)
    spoke_at = lax.div(me, CORES * RING) * CORES + core

    def ring_peer(step):
        at = lax.rem(ring_at + step, RING)
        return at, me + (at - ring_at) * CORES

    def spoke_peer(step):
        at = lax.rem(spoke_at + step, spokes)
        return at, (lax.div(at, CORES) * RING + ring_at) * CORES + lax.rem(at, CORES)

    ring_steps = far_first(RING)
    spoke_steps = far_first(spokes)
    mesh_steps = far_first(columns)
    barrier = pltpu.get_barrier_semaphore()

    def ring_turn(turn):
        step = lax.div(RING - turn, 2) * (1 - 2 * lax.rem(turn, 2))
        return lax.rem(ring_at + step + RING, RING)

    def greet(peer):
        pl.semaphore_signal(barrier, inc=1, device_id={"grid": peer}, device_id_type=MESH)

    def greet_ring(turn, carry):
        at = ring_turn(turn)
        for spoke in range(spokes):
            greet((spoke // CORES * RING + at) * CORES + spoke % CORES)
        return carry

    lax.fori_loop(0, RING - 1, greet_ring, 0)
    for step in spoke_steps:
        greet(spoke_peer(step)[1])
    for step in mesh_steps:
        to = {"mesh": lax.rem(my + step, columns)}
        pl.semaphore_signal(barrier, inc=1, device_id=to, device_id_type=MESH)

    shift = (nodes * columns).bit_length() - 1
    upto = hot(iota((slots, slots), 0) <= iota((slots, slots), 1))
    ready(dst, src, ef, w_edge, feat, w_grid)
    target = jnp.broadcast_to(dst[...], (8, slots))
    edge_at = iota((8, slots), 1)
    last = jnp.max(jnp.where(target > 0, edge_at, -1), axis=1, keepdims=True)
    live = edge_at <= last
    fresh = live & ((edge_at == 0) | (target != pltpu.roll(target, 1, 1)))
    fresh_f = jnp.where(fresh, 1.0, 0.0)
    band = lax.shift_right_logical(target, shift)
    low = band & (CORES - 1)
    along = lax.shift_right_logical(band, LOG_CORES) & (RING - 1)
    across = lax.shift_right_logical(band, LOG_CORES + LOG_RING)
    owner = jnp.where(live, along * spokes + across * CORES + low, -1)
    of_owner = owner[0:1] == iota((groups, slots), 0)
    counted = dot(jnp.where(of_owner, fresh_f[0:1], 0.0).astype(BF16), upto)
    rank = jnp.sum(jnp.where(of_owner, counted, 0.0), axis=0, keepdims=True)
    row_of_edge = jnp.where(
        live[0:1], (rank - 1.0) * groups + owner[0:1].astype(F32), -1.0
    )
    picking = hot_rows(row_of_edge, CAP * groups)
    local_f = jnp.where(fresh, (target & (nodes - 1)).astype(F32), 0.0)
    ids = dot_nt(picking, jnp.broadcast_to(local_f[0:1], (128, slots)).astype(BF16))
    lane = iota((groups, 128), 1)
    keys = ids[0:groups]
    for j in range(1, CAP):
        keys = jnp.where(lane & (CAP - 1) == j, ids[j * groups : (j + 1) * groups], keys)
    id_send[...] = keys.reshape(RING, spokes, 1, 128)

    e1, e2, e3 = parts(ef[...])
    w1, w2, w3 = parts(w_edge[...])
    e_all = jnp.concatenate([e1, e1, e2, e1, e2, e3], axis=0).astype(BF16)
    w_all = jnp.concatenate([w1, w2, w1, w3, w2, w1], axis=0).astype(BF16)
    edge_latent = silu(dot_tn(e_all, w_all)).astype(BF16)
    grid_latent = silu(dot_tn(feat[...], w_grid[...])).astype(BF16)
    from_node = jnp.transpose(jnp.broadcast_to(src[...], (128, slots)).astype(F32)).astype(BF16)
    lane_at = iota((slots, 128), 1).astype(F32)
    one, none = jnp.ones((slots, 128), BF16), jnp.zeros((slots, 128), BF16)
    gathering = [
        jnp.where(from_node == (lane_at + float(at)).astype(BF16), one, none)
        for at in range(0, g_nodes, 128)
    ]
    ready(w_mi)
    w_mi[width : width + g_nodes] = dot(grid_latent, w_mi[width:]).astype(BF16)
    both = jnp.concatenate([edge_latent] + gathering, axis=1)
    hidden = silu(dot(both, w_mi[0 : width + g_nodes])).astype(BF16)
    ready(w_mo, gain_m)
    for there in (omap, lat, w_ni, w_no, gain_n):
        loads[id(there)].start()
    mixed = dot(hidden, w_mo[...])
    message[...] = (edge_latent.astype(F32) + normed(mixed) * gain_m[...]).astype(BF16)
    summed = dot(picking, message[...])
    quarters = width // 128
    for j in range(CAP):
        for c in range(quarters):
            wide[pl.ds(j * quarters + c, groups, stride=TILE), :] = summed[
                j * groups : (j + 1) * groups, c * 128 : (c + 1) * 128
            ]
    send[...] = wide[...].astype(BF16).reshape(groups, TILE, 128)
    pl.semaphore_wait(barrier, groups + columns - 2)

    def remote(outgoing, incoming, sems, to):
        return pltpu.make_async_remote_copy(
            src_ref=outgoing,
            dst_ref=incoming,
            send_sem=sems.at[0],
            recv_sem=sems.at[1],
            device_id=to,
            device_id_type=MESH,
        )

    def along_ring(outgoing, incoming, sems):
        for step in ring_steps:
            at, peer = ring_peer(step)
            remote(outgoing.at[at], incoming.at[ring_at], sems, {"grid": peer}).start()
        incoming[pl.ds(ring_at, 1)] = outgoing[pl.ds(ring_at, 1)]

    def along_spokes(outgoing, incoming, sems):
        for step in spoke_steps:
            at, peer = spoke_peer(step)
            remote(outgoing.at[:, at], incoming.at[spoke_at], sems, {"grid": peer}).start()
        kept = outgoing[:, pl.ds(spoke_at, 1)]
        incoming[pl.ds(spoke_at, 1)] = kept.reshape((1, RING) + kept.shape[2:])

    def along_mesh(outgoing, incoming, sems):
        def rows(at):
            return pl.ds(pl.multiple_of(at * share, share), share)

        for step in mesh_steps:
            peer = lax.rem(my + step, columns)
            remote(outgoing.at[rows(peer)], incoming.at[rows(my)], sems, {"mesh": peer}).start()
        incoming[rows(my), :] = outgoing[rows(my), :]

    def drain(sem, ref):
        pltpu.make_async_copy(ref, ref, sem).wait()

    slot = spoke_at * RING + ring_at

    along_ring(id_send, id_passed, id_sems)

    def pay_ring(turn, carry):
        at = ring_turn(turn)
        for spoke in range(spokes):
            peer = (spoke // CORES * RING + at) * CORES + spoke % CORES
            block = send.at[at * spokes + spoke]
            remote(block, recv.at[slot], pay_sems, {"grid": peer}).start()
        return carry

    lax.fori_loop(0, RING - 1, pay_ring, 0)
    for step in spoke_steps:
        at, peer = spoke_peer(step)
        block = send.at[ring_at * spokes + at]
        remote(block, recv.at[slot], pay_sems, {"grid": peer}).start()
    recv[pl.ds(slot, 1)] = send[pl.ds(ring_at * spokes + spoke_at, 1)]
    drain(id_sems.at[1], id_passed.at[pl.ds(0, RING - 1)])
    along_spokes(id_passed, id_recv, id_sems_2)

    share = nodes // columns
    node_shift = nodes.bit_length() - 1
    ready(omap)
    held = omap[...]
    home = lax.shift_right_logical(held, node_shift) & (columns - 1)
    at_home = home == iota((columns, nodes), 0)
    before = hot(iota((nodes, nodes), 0) <= iota((nodes, nodes), 1))
    nth = dot(hot(at_home), before)
    leave = jnp.sum(
        jnp.where(at_home, nth + (iota((columns, nodes), 0) * share - 1).astype(F32), 0.0),
        axis=0,
        keepdims=True,
    )
    leaving = hot_rows(leave, nodes)
    node_hot_t = hot((held & (nodes - 1)) == iota((nodes, nodes), 0))
    place_send[...] = dot_nt(leaving, node_hot_t).astype(BF16)
    position = dot_nt(
        leaving, jnp.broadcast_to(iota((1, nodes), 1).astype(F32), (128, nodes)).astype(BF16)
    )

    along_mesh(place_send, place_recv, place_sems)

    ready(lat, w_ni)
    lat_rows = dot(leaving, lat[...])
    pre = dot(lat_rows.astype(BF16), w_ni[0:width])
    drain(id_sems_2.at[1], id_recv.at[pl.ds(0, spokes - 1)])
    lines = id_recv[...].reshape(groups, 128)
    senders = 128 // CAP
    mine = lax.shift_right_logical(iota((senders, 128), 1), CAP.bit_length() - 1) == iota(
        (senders, 128), 0
    )
    for b in range(groups // senders):
        key = jnp.sum(
            jnp.where(mine, lines[b * senders : (b + 1) * senders], 0.0), axis=0, keepdims=True
        )
        adding[:, b * 128 : (b + 1) * 128] = hot(key == position)
    drain(place_sems.at[1], place_recv.at[pl.ds(0, nodes - share)])
    placing = jnp.transpose(place_recv[...].astype(F32)).astype(BF16)
    ready(w_no, gain_n)

    drain(pay_sems.at[1], recv.at[pl.ds(0, groups - 1)])
    wide[...] = recv[...].reshape(groups * TILE, 128).astype(F32)
    rows = jnp.concatenate(
        [wide[pl.ds(c, CAP * groups, stride=quarters), :].astype(BF16) for c in range(quarters)],
        axis=1,
    )
    summed_low = dot(adding[...], rows).astype(BF16)
    hidden_node = silu(pre + dot(summed_low, w_ni[width:])).astype(BF16)
    mixed_node = dot(hidden_node, w_no[...])
    row_send[...] = (lat_rows + normed(mixed_node) * gain_n[...]).astype(BF16)

    along_mesh(row_send, row_recv, row_sems)
    drain(id_sems.at[0], id_send.at[pl.ds(0, RING - 1)])
    drain(id_sems_2.at[0], id_recv.at[pl.ds(0, spokes - 1)])
    drain(place_sems.at[0], place_send.at[pl.ds(0, nodes - share)])
    drain(pay_sems.at[0], send.at[pl.ds(0, groups - 1)])
    drain(row_sems.at[1], row_recv.at[pl.ds(0, nodes - share)])
    out_ref[...] = dot(placing, row_recv[...]).astype(BF16)
    drain(row_sems.at[0], row_send.at[pl.ds(0, nodes - share)])


def shards(
    grid_features,
    edge_feats,
    edge_src,
    edge_dst,
    edge_count,
    mesh_lat,
    owner_map,
    w_grid,
    w_edge,
    w_msg_in,
    w_msg_out,
    gain_msg,
    w_node_in,
    w_node_out,
    gain_node,
):
    groups, columns = lax.axis_size("grid"), lax.axis_size("mesh")
    nodes, width = mesh_lat.shape
    operands = (
        grid_features,
        edge_feats,
        edge_src.reshape(1, -1),
        edge_dst.reshape(1, -1),
        mesh_lat,
        owner_map.reshape(1, -1),
        w_grid,
        w_edge,
        w_msg_in,
        w_msg_out,
        gain_msg.reshape(1, -1),
        w_node_in,
        w_node_out,
        gain_node.reshape(1, -1),
    )
    copies = [pltpu.VMEM(v.shape, v.dtype) for v in operands]
    rows = groups * TILE
    spokes = groups // RING
    return pl.pallas_call(
        functools.partial(kernel, groups, columns),
        out_shape=pltpu.VMEM((nodes, width), BF16),
        in_specs=[pl.BlockSpec(memory_space=pl.ANY)] * len(operands),
        out_specs=pl.BlockSpec(memory_space=pltpu.VMEM),
        scratch_shapes=copies
        + [
            pltpu.VMEM((edge_dst.shape[0], width), BF16),
            pltpu.VMEM((rows, 128), F32),
            pltpu.VMEM((groups, TILE, 128), BF16),
            pltpu.VMEM((groups, TILE, 128), BF16),
            pltpu.VMEM((RING, spokes, 1, 128), F32),
            pltpu.VMEM((RING, spokes, 1, 128), F32),
            pltpu.VMEM((spokes, RING, 1, 128), F32),
            pltpu.VMEM((nodes, CAP * groups), BF16),
            pltpu.VMEM((nodes, nodes), BF16),
            pltpu.VMEM((nodes, nodes), BF16),
            pltpu.VMEM((nodes, width), BF16),
            pltpu.VMEM((nodes, width), BF16),
            pltpu.SemaphoreType.DMA((len(operands),)),
        ]
        + [pltpu.SemaphoreType.DMA((2,))] * 5,
        compiler_params=pltpu.CompilerParams(
            collective_id=0, has_side_effects=True, vmem_limit_bytes=56 * 1024 * 1024
        ),
        cost_estimate=pl.CostEstimate(
            flops=2_000_000_000, bytes_accessed=5_000_000, transcendentals=800_000
        ),
        name="encode",
    )(*operands)


def solution(mesh):
    placed = (
        P(None, ("grid", "mesh")),
        P(None, ("grid", "mesh")),
        P(("grid", "mesh")),
        P(("grid", "mesh")),
        P(("grid", "mesh")),
        P(("grid", "mesh"), None),
        P(("grid", "mesh")),
        P(),
        P(),
        P(),
        P(),
        P(),
        P(),
        P(),
        P(),
    )
    return jax.shard_map(
        shards, mesh=mesh, in_specs=placed, out_specs=P(("grid", "mesh"), None), check_vma=False
    )
```

```python
import functools

import jax
import jax.numpy as jnp
from jax import lax
from jax.experimental import pallas as pl
from jax.experimental.pallas import tpu as pltpu
from jax.sharding import PartitionSpec as P

F32 = jnp.float32
BF16 = jnp.bfloat16
MESH = pl.DeviceIdType.MESH
CAP = 4
TILE = 16
LOG_CORES = 1
LOG_RING = 3
CORES = 1 << LOG_CORES
RING = 1 << LOG_RING


def far_first(size):
    return sorted(range(1, size), key=lambda step: -min(step, size - step))


def silu(v):
    half = 0.5 * v
    return half + half * jnp.tanh(half)


def normed(v):
    mean = jnp.mean(v, axis=-1, keepdims=True)
    centred = v - mean
    variance = jnp.mean(centred * centred, axis=-1, keepdims=True)
    return centred * lax.rsqrt(variance + 1e-05)


def dot(a, b):
    return lax.dot_general(a, b, (((1,), (0,)), ((), ())), preferred_element_type=F32)


def dot_tn(a, b):
    return lax.dot_general(a, b, (((0,), (0,)), ((), ())), preferred_element_type=F32)


def dot_nt(a, b):
    return lax.dot_general(a, b, (((1,), (1,)), ((), ())), preferred_element_type=F32)


def iota(shape, dim):
    return lax.broadcasted_iota(jnp.int32, shape, dim)


def hot(mask):
    return jnp.where(mask, 1.0, 0.0).astype(BF16)


def hot_rows(row, count):
    at = iota((count, row.shape[1]), 0).astype(F32).astype(BF16)
    there = jnp.broadcast_to(row.astype(BF16), at.shape)
    return jnp.where(there == at, jnp.ones_like(at), jnp.zeros_like(at))


def parts(v):
    a = v.astype(BF16).astype(F32)
    rest = v - a
    b = rest.astype(BF16).astype(F32)
    return a, b, rest - b


def kernel(
    groups,
    columns,
    feat_h,
    ef_h,
    src_h,
    dst_h,
    lat_h,
    map_h,
    w_grid_h,
    w_edge_h,
    w_mi_h,
    w_mo_h,
    gain_m_h,
    w_ni_h,
    w_no_h,
    gain_n_h,
    out_ref,
    feat,
    ef,
    src,
    dst,
    lat,
    omap,
    w_grid,
    w_edge,
    w_mi,
    w_mo,
    gain_m,
    w_ni,
    w_no,
    gain_n,
    message,
    wide,
    send,
    recv,
    id_send,
    id_passed,
    id_recv,
    adding,
    place_send,
    place_recv,
    row_send,
    row_recv,
    load_sem,
    id_sems,
    id_sems_2,
    place_sems,
    pay_sems,
    row_sems,
):
    width = w_mo.shape[0]
    slots = dst.shape[1]
    nodes = omap.shape[1]
    g_nodes = feat.shape[1]
    me = lax.axis_index("grid")
    my = lax.axis_index("mesh")

    loads = {}
    pairs = (
        (dst_h, dst),
        (src_h, src),
        (ef_h, ef),
        (w_edge_h, w_edge),
        (feat_h, feat),
        (w_grid_h, w_grid),
        (w_mi_h, w_mi),
        (w_mo_h, w_mo),
        (gain_m_h, gain_m),
        (map_h, omap),
        (lat_h, lat),
        (w_ni_h, w_ni),
        (w_no_h, w_no),
        (gain_n_h, gain_n),
    )
    for at, (here, there) in enumerate(pairs):
        loads[id(there)] = pltpu.make_async_copy(here, there, load_sem.at[at])
    for there in (dst, src, ef, w_edge, feat, w_grid):
        loads[id(there)].start()

    def ready(*refs):
        for ref in refs:
            loads[id(ref)].wait()

    depth = groups // CORES // RING
    spokes = depth * CORES
    core = lax.rem(me, CORES)
    ring_at = lax.rem(lax.div(me, CORES), RING)
    spoke_at = lax.div(me, CORES * RING) * CORES + core

    def ring_peer(step):
        at = lax.rem(ring_at + step, RING)
        return at, me + (at - ring_at) * CORES

    def spoke_peer(step):
        at = lax.rem(spoke_at + step, spokes)
        return at, (lax.div(at, CORES) * RING + ring_at) * CORES + lax.rem(at, CORES)

    ring_steps = far_first(RING)
    spoke_steps = far_first(spokes)
    mesh_steps = far_first(columns)
    barrier = pltpu.get_barrier_semaphore()

    def ring_turn(turn):
        step = lax.div(RING - turn, 2) * (1 - 2 * lax.rem(turn, 2))
        return lax.rem(ring_at + step + RING, RING)

    def greet(peer):
        pl.semaphore_signal(barrier, inc=1, device_id={"grid": peer}, device_id_type=MESH)

    def greet_ring(turn, carry):
        at = ring_turn(turn)
        for spoke in range(spokes):
            greet((spoke // CORES * RING + at) * CORES + spoke % CORES)
        return carry

    lax.fori_loop(0, RING - 1, greet_ring, 0)
    for step in spoke_steps:
        greet(spoke_peer(step)[1])
    for step in mesh_steps:
        to = {"mesh": lax.rem(my + step, columns)}
        pl.semaphore_signal(barrier, inc=1, device_id=to, device_id_type=MESH)

    for there in (w_mi, w_mo, gain_m):
        loads[id(there)].start()

    shift = (nodes * columns).bit_length() - 1
    upto = hot(iota((slots, slots), 0) <= iota((slots, slots), 1))
    ready(dst, src, ef, w_edge, feat, w_grid)
    target = jnp.broadcast_to(dst[...], (8, slots))
    edge_at = iota((8, slots), 1)
    last = jnp.max(jnp.where(target > 0, edge_at, -1), axis=1, keepdims=True)
    live = edge_at <= last
    fresh = live & ((edge_at == 0) | (target != pltpu.roll(target, 1, 1)))
    fresh_f = jnp.where(fresh, 1.0, 0.0)
    band = lax.shift_right_logical(target, shift)
    low = band & (CORES - 1)
    along = lax.shift_right_logical(band, LOG_CORES) & (RING - 1)
    across = lax.shift_right_logical(band, LOG_CORES + LOG_RING)
    owner = jnp.where(live, along * spokes + across * CORES + low, -1)
    of_owner = owner[0:1] == iota((groups, slots), 0)
    counted = dot(jnp.where(of_owner, fresh_f[0:1], 0.0).astype(BF16), upto)
    rank = jnp.sum(jnp.where(of_owner, counted, 0.0), axis=0, keepdims=True)
    row_of_edge = jnp.where(
        live[0:1], (rank - 1.0) * groups + owner[0:1].astype(F32), -1.0
    )
    picking = hot_rows(row_of_edge, CAP * groups)
    local_f = jnp.where(fresh, (target & (nodes - 1)).astype(F32), 0.0)
    ids = dot_nt(picking, jnp.broadcast_to(local_f[0:1], (128, slots)).astype(BF16))
    lane = iota((groups, 128), 1)
    keys = ids[0:groups]
    for j in range(1, CAP):
        keys = jnp.where(lane & (CAP - 1) == j, ids[j * groups : (j + 1) * groups], keys)
    id_send[...] = keys.reshape(RING, spokes, 1, 128)

    e1, e2, e3 = parts(ef[...])
    w1, w2, w3 = parts(w_edge[...])
    e_all = jnp.concatenate([e1, e1, e2, e1, e2, e3], axis=0).astype(BF16)
    w_all = jnp.concatenate([w1, w2, w1, w3, w2, w1], axis=0).astype(BF16)
    edge_latent = silu(dot_tn(e_all, w_all)).astype(BF16)
    grid_latent = silu(dot_tn(feat[...], w_grid[...])).astype(BF16)
    from_node = jnp.transpose(jnp.broadcast_to(src[...], (128, slots)).astype(F32)).astype(BF16)
    lane_at = iota((slots, 128), 1).astype(F32)
    one, none = jnp.ones((slots, 128), BF16), jnp.zeros((slots, 128), BF16)
    gathering = [
        jnp.where(from_node == (lane_at + float(at)).astype(BF16), one, none)
        for at in range(0, g_nodes, 128)
    ]
    ready(w_mi)
    w_mi[width : width + g_nodes] = dot(grid_latent, w_mi[width:]).astype(BF16)
    both = jnp.concatenate([edge_latent] + gathering, axis=1)
    hidden = silu(dot(both, w_mi[0 : width + g_nodes])).astype(BF16)
    ready(w_mo, gain_m)
    for there in (omap, lat, w_ni, w_no, gain_n):
        loads[id(there)].start()
    mixed = dot(hidden, w_mo[...])
    message[...] = (edge_latent.astype(F32) + normed(mixed) * gain_m[...]).astype(BF16)
    summed = dot(picking, message[...])
    quarters = width // 128
    for j in range(CAP):
        for c in range(quarters):
            wide[pl.ds(j * quarters + c, groups, stride=TILE), :] = summed[
                j * groups : (j + 1) * groups, c * 128 : (c + 1) * 128
            ]
    send[...] = wide[...].astype(BF16).reshape(groups, TILE, 128)
    pl.semaphore_wait(barrier, groups + columns - 2)

    def remote(outgoing, incoming, sems, to):
        return pltpu.make_async_remote_copy(
            src_ref=outgoing,
            dst_ref=incoming,
            send_sem=sems.at[0],
            recv_sem=sems.at[1],
            device_id=to,
            device_id_type=MESH,
        )

    def along_ring(outgoing, incoming, sems):
        for step in ring_steps:
            at, peer = ring_peer(step)
            remote(outgoing.at[at], incoming.at[ring_at], sems, {"grid": peer}).start()
        incoming[pl.ds(ring_at, 1)] = outgoing[pl.ds(ring_at, 1)]

    def along_spokes(outgoing, incoming, sems):
        for step in spoke_steps:
            at, peer = spoke_peer(step)
            remote(outgoing.at[:, at], incoming.at[spoke_at], sems, {"grid": peer}).start()
        kept = outgoing[:, pl.ds(spoke_at, 1)]
        incoming[pl.ds(spoke_at, 1)] = kept.reshape((1, RING) + kept.shape[2:])

    def along_mesh(outgoing, incoming, sems):
        def rows(at):
            return pl.ds(pl.multiple_of(at * share, share), share)

        for step in mesh_steps:
            peer = lax.rem(my + step, columns)
            remote(outgoing.at[rows(peer)], incoming.at[rows(my)], sems, {"mesh": peer}).start()
        incoming[rows(my), :] = outgoing[rows(my), :]

    def drain(sem, ref):
        pltpu.make_async_copy(ref, ref, sem).wait()

    slot = spoke_at * RING + ring_at

    along_ring(id_send, id_passed, id_sems)

    spoke_order = []
    for step in [0] + spoke_steps:
        spoke = lax.rem(spoke_at + step, spokes)
        first = lax.div(spoke, CORES) * (RING * CORES) + lax.rem(spoke, CORES)
        spoke_order.append((spoke, first))

    def pay_ring(turn, carry):
        at = ring_turn(turn)
        for spoke, first in spoke_order:
            block = send.at[at * spokes + spoke]
            peer = {"grid": first + at * CORES}
            remote(block, recv.at[slot], pay_sems, peer).start()
        return carry

    lax.fori_loop(0, RING - 1, pay_ring, 0)
    for step in spoke_steps:
        at, peer = spoke_peer(step)
        block = send.at[ring_at * spokes + at]
        remote(block, recv.at[slot], pay_sems, {"grid": peer}).start()
    recv[pl.ds(slot, 1)] = send[pl.ds(ring_at * spokes + spoke_at, 1)]
    drain(id_sems.at[1], id_passed.at[pl.ds(0, RING - 1)])
    along_spokes(id_passed, id_recv, id_sems_2)

    share = nodes // columns
    node_shift = nodes.bit_length() - 1
    ready(omap)
    held = omap[...]
    home = lax.shift_right_logical(held, node_shift) & (columns - 1)
    at_home = home == iota((columns, nodes), 0)
    before = hot(iota((nodes, nodes), 0) <= iota((nodes, nodes), 1))
    nth = dot(hot(at_home), before)
    leave = jnp.sum(
        jnp.where(at_home, nth + (iota((columns, nodes), 0) * share - 1).astype(F32), 0.0),
        axis=0,
        keepdims=True,
    )
    leaving = hot_rows(leave, nodes)
    node_hot_t = hot((held & (nodes - 1)) == iota((nodes, nodes), 0))
    place_send[...] = dot_nt(leaving, node_hot_t).astype(BF16)
    position = dot_nt(
        leaving, jnp.broadcast_to(iota((1, nodes), 1).astype(F32), (128, nodes)).astype(BF16)
    )

    along_mesh(place_send, place_recv, place_sems)

    ready(lat, w_ni)
    lat_rows = dot(leaving, lat[...])
    pre = dot(lat_rows.astype(BF16), w_ni[0:width])
    drain(id_sems_2.at[1], id_recv.at[pl.ds(0, spokes - 1)])
    lines = id_recv[...].reshape(groups, 128)
    senders = 128 // CAP
    mine = lax.shift_right_logical(iota((senders, 128), 1), CAP.bit_length() - 1) == iota(
        (senders, 128), 0
    )
    for b in range(groups // senders):
        key = jnp.sum(
            jnp.where(mine, lines[b * senders : (b + 1) * senders], 0.0), axis=0, keepdims=True
        )
        adding[:, b * 128 : (b + 1) * 128] = hot(key == position)
    drain(place_sems.at[1], place_recv.at[pl.ds(0, nodes - share)])
    placing = jnp.transpose(place_recv[...].astype(F32)).astype(BF16)
    ready(w_no, gain_n)

    drain(pay_sems.at[1], recv.at[pl.ds(0, groups - 1)])
    wide[...] = recv[...].reshape(groups * TILE, 128).astype(F32)
    rows = jnp.concatenate(
        [wide[pl.ds(c, CAP * groups, stride=quarters), :].astype(BF16) for c in range(quarters)],
        axis=1,
    )
    summed_low = dot(adding[...], rows).astype(BF16)
    hidden_node = silu(pre + dot(summed_low, w_ni[width:])).astype(BF16)
    mixed_node = dot(hidden_node, w_no[...])
    row_send[...] = (lat_rows + normed(mixed_node) * gain_n[...]).astype(BF16)

    along_mesh(row_send, row_recv, row_sems)
    drain(id_sems.at[0], id_send.at[pl.ds(0, RING - 1)])
    drain(id_sems_2.at[0], id_recv.at[pl.ds(0, spokes - 1)])
    drain(place_sems.at[0], place_send.at[pl.ds(0, nodes - share)])
    drain(pay_sems.at[0], send.at[pl.ds(0, groups - 1)])
    drain(row_sems.at[1], row_recv.at[pl.ds(0, nodes - share)])
    out_ref[...] = dot(placing, row_recv[...]).astype(BF16)
    drain(row_sems.at[0], row_send.at[pl.ds(0, nodes - share)])


def shards(
    grid_features,
    edge_feats,
    edge_src,
    edge_dst,
    edge_count,
    mesh_lat,
    owner_map,
    w_grid,
    w_edge,
    w_msg_in,
    w_msg_out,
    gain_msg,
    w_node_in,
    w_node_out,
    gain_node,
):
    groups, columns = lax.axis_size("grid"), lax.axis_size("mesh")
    nodes, width = mesh_lat.shape
    operands = (
        grid_features,
        edge_feats,
        edge_src.reshape(1, -1),
        edge_dst.reshape(1, -1),
        mesh_lat,
        owner_map.reshape(1, -1),
        w_grid,
        w_edge,
        w_msg_in,
        w_msg_out,
        gain_msg.reshape(1, -1),
        w_node_in,
        w_node_out,
        gain_node.reshape(1, -1),
    )
    copies = [pltpu.VMEM(v.shape, v.dtype) for v in operands]
    rows = groups * TILE
    spokes = groups // RING
    return pl.pallas_call(
        functools.partial(kernel, groups, columns),
        out_shape=pltpu.VMEM((nodes, width), BF16),
        in_specs=[pl.BlockSpec(memory_space=pl.ANY)] * len(operands),
        out_specs=pl.BlockSpec(memory_space=pltpu.VMEM),
        scratch_shapes=copies
        + [
            pltpu.VMEM((edge_dst.shape[0], width), BF16),
            pltpu.VMEM((rows, 128), F32),
            pltpu.VMEM((groups, TILE, 128), BF16),
            pltpu.VMEM((groups, TILE, 128), BF16),
            pltpu.VMEM((RING, spokes, 1, 128), F32),
            pltpu.VMEM((RING, spokes, 1, 128), F32),
            pltpu.VMEM((spokes, RING, 1, 128), F32),
            pltpu.VMEM((nodes, CAP * groups), BF16),
            pltpu.VMEM((nodes, nodes), BF16),
            pltpu.VMEM((nodes, nodes), BF16),
            pltpu.VMEM((nodes, width), BF16),
            pltpu.VMEM((nodes, width), BF16),
            pltpu.SemaphoreType.DMA((len(operands),)),
        ]
        + [pltpu.SemaphoreType.DMA((2,))] * 5,
        compiler_params=pltpu.CompilerParams(
            collective_id=0, has_side_effects=True, vmem_limit_bytes=56 * 1024 * 1024
        ),
        cost_estimate=pl.CostEstimate(
            flops=2_000_000_000, bytes_accessed=5_000_000, transcendentals=800_000
        ),
        name="encode",
    )(*operands)


def solution(mesh):
    placed = (
        P(None, ("grid", "mesh")),
        P(None, ("grid", "mesh")),
        P(("grid", "mesh")),
        P(("grid", "mesh")),
        P(("grid", "mesh")),
        P(("grid", "mesh"), None),
        P(("grid", "mesh")),
        P(),
        P(),
        P(),
        P(),
        P(),
        P(),
        P(),
        P(),
    )
    return jax.shard_map(
        shards, mesh=mesh, in_specs=placed, out_specs=P(("grid", "mesh"), None), check_vma=False
    )
```
